32 devices in a mesh: dc: 8 (over y, x, core), tp: 4 (over z).
Axes of the slice: x: 2, y: 2, z: 4, core: 2. Of those that a mesh axis runs over, the one named last changes fastest.
Arguments:
- queries: bfloat16 [1536, 1024], P('dc', 'tp'), may hold values from -15 to 15
- keys: bfloat16 [1536, 256], P('dc'), may hold values from -4.5 to 4.5
- values: bfloat16 [1536, 256], P('dc'), may hold values from -5 to 5
- lengths: int32 [24], replicated, may hold values from 1 to 1152, 1536 in all
- mlp_owner: int32 [1536], replicated, may hold values from 0 to 7, as said below
- out_weight: bfloat16 [1024, 4096], P('tp'), may hold values from -0.1875 to 0.1875
- residual: bfloat16 [1536, 4096], P(('dc', 'tp')), may hold values from -3 to 3
Outputs:
- hidden: bfloat16 [1536, 4096], P(('dc', 'tp'))
The draws below stay inside these ranges and needn't reach their ends.
Inputs may be any that keep to these rules, and one draw needn't show every extreme that they name: `mlp_owner`: the tokens of any one slab of 192 positions send at most 48 tokens to one owner, and every owner receives exactly 192 tokens.
All inputs are finite; a program needn't handle non-finite values.
Results may differ from the reference program's by a relative error of at most 0.013.
Values may be sent and summed in bfloat16 or wider, within the bound.
A program may use at most 128 MiB of HBM per device.

```python
import math
import jax
import jax.numpy as jnp
import numpy as np
from jax import lax

D = 4096
HEAD_SIZE = 128
GROUP = 4
DOCS = 24
TOK_DEV = 192
HQ = 8
KEY_VALUE_HEADS = 2
ROW_TOKENS = 1536
MOST = 1152
N_DC = 8


def draw_queries(key, part):
    normal_key = jax.random.fold_in(jax.random.fold_in(key, 1), 0)
    base_offset = jax.random.normal(normal_key, (ROW_TOKENS, HQ * HEAD_SIZE), jnp.float32) * 3.0
    base_offset = jnp.clip(base_offset, -15.0, 15.0)
    return base_offset.astype(jnp.bfloat16)


def draw_keys(key, part):
    base_offset = jax.random.normal(jax.random.fold_in(key, 2), (ROW_TOKENS, KEY_VALUE_HEADS * HEAD_SIZE), jnp.float32)
    base_offset = jnp.clip(base_offset, -4.5, 4.5)
    return base_offset.astype(jnp.bfloat16)


def draw_mlp_owner(key, part):
    perm_key, shuffle_key = jax.random.split(jax.random.fold_in(key, 3))
    owners = jnp.arange(N_DC, dtype=jnp.int32)
    source = owners[:, None]
    target = owners[None, :]
    remainder = TOK_DEV % N_DC
    counts = TOK_DEV // N_DC + ((target - source) % N_DC < remainder).astype(jnp.int32)
    mapping = jax.random.permutation(perm_key, N_DC).astype(jnp.int32)
    first = (target == mapping[:, None]).astype(jnp.int32)
    second = (target == (mapping[:, None] + 1) % N_DC).astype(jnp.int32)
    counts = counts + TOK_DEV // N_DC * (first - second)
    labels = jax.vmap(lambda row: jnp.repeat(owners, row, total_repeat_length=TOK_DEV))(counts)
    shuffle_keys = jax.random.split(shuffle_key, N_DC)
    mixed = jax.vmap(lambda single, row: jax.random.permutation(single, row))(shuffle_keys, labels)
    return mixed.reshape(ROW_TOKENS).astype(jnp.int32)


def shard_levels(key, extent, pieces, least, largest):
    loudness = 1.0
    for axis_at, blocks in pieces:
        steps = jax.random.uniform(jax.random.fold_in(jax.random.fold_in(key, 6), axis_at), (blocks,), jnp.float32, least / len(pieces), largest / len(pieces))
        loudness = loudness * jnp.repeat(jnp.exp(steps), extent[axis_at] // blocks).reshape((-1,) + (1,) * (len(extent) - 1 - axis_at))
    return loudness


def length_profile(amount, total, reach, skew):
    portions = [(1 << 20) // math.isqrt(rank ** skew) + 1 for rank in range(2, amount + 1)]
    rest, given = total - reach - (amount - 1), [1] * (amount - 1)
    while rest > 0:
        free = [i for i in range(amount - 1) if given[i] < reach]
        mass, remaining = sum([portions[i] for i in free]), rest
        for i in free:
            more = min(reach - given[i], max(1, remaining * portions[i] // mass), rest)
            given[i] = given[i] + more
            rest = rest - more
    return np.array([reach] + given)


def ragged(rng, count, total, reach, slope):
    if count == 2:
        one = jax.random.randint(rng, (), max(1, total - reach), min(reach, total - 1) + 1)
        return jnp.stack([one, total - one])
    sizes = jnp.asarray(length_profile(count, total, reach, slope), jnp.int32)
    couples = (count - 1) // 2
    donor, sink = sizes[1:1 + 2 * couples:2], sizes[2:2 + 2 * couples:2]
    slack = jnp.minimum(donor - 1, reach - sink)
    moved = jax.random.randint(jax.random.fold_in(rng, 1), (couples,), 0, 1 << 20) % (slack + 1)
    sizes = sizes.at[1:1 + 2 * couples:2].set(donor - moved).at[2:2 + 2 * couples:2].set(sink + moved)
    return sizes[jax.random.permutation(jax.random.fold_in(rng, 2), count)]


def centred(own_key, extent, scale, most, shards=(), held_as=jnp.bfloat16):
    entries = jax.random.normal(own_key, extent, jnp.float32) * scale
    if len(shards) > 0:
        entries = shard_levels(own_key, extent, shards, -0.22, 0.18) * entries
    return jnp.clip(entries, min=-most, max=most).astype(held_as)


def setup_inputs(seed: int = 0) -> dict:
    splits = jax.random.split(jax.random.key(seed), 8)
    queries = draw_queries(jax.random.fold_in(splits[7], 71), 0)
    keys = draw_keys(jax.random.fold_in(splits[7], 71), 0)
    values = centred(splits[2], (ROW_TOKENS, KEY_VALUE_HEADS * HEAD_SIZE), 1.0, 5.0, ((0, 8),))
    lengths = ragged(splits[3], DOCS, ROW_TOKENS, MOST, 2).astype(jnp.int32)
    mlp_owner = draw_mlp_owner(jax.random.fold_in(splits[7], 71), 0)
    out_weight = centred(splits[5], (HQ * HEAD_SIZE, D), (HQ * HEAD_SIZE) ** -0.5, 0.1875, ((0, 4),))
    residual = centred(splits[6], (ROW_TOKENS, D), 0.5, 3.0, ((0, 32),))
    return dict(queries=queries, keys=keys, values=values, lengths=lengths, mlp_owner=mlp_owner, out_weight=out_weight, residual=residual)


def doc_index(positions, doc_ends):
    return jnp.sum((positions[:, None] >= doc_ends[None, :]).astype(jnp.int32), axis=1)


def reference(queries, keys, values, lengths, mlp_owner, out_weight, residual):
    doc_ends = jnp.cumsum(lengths).astype(jnp.int32)
    positions = jnp.arange(ROW_TOKENS, dtype=jnp.int32)
    documents = doc_index(positions, doc_ends)
    block_rows = math.gcd(ROW_TOKENS, 512)
    block_total = ROW_TOKENS // block_rows
    scale = HEAD_SIZE ** -0.5

    def one_head(head):
        query_cols = lax.dynamic_slice_in_dim(queries, head * HEAD_SIZE, HEAD_SIZE, 1)
        shared = head // GROUP
        key_cols = lax.dynamic_slice_in_dim(keys, shared * HEAD_SIZE, HEAD_SIZE, 1)
        value_cols = lax.dynamic_slice_in_dim(values, shared * HEAD_SIZE, HEAD_SIZE, 1)

        def one_block(block):
            offset = block * block_rows
            query_rows = lax.dynamic_slice_in_dim(query_cols, offset, block_rows, 0)
            query_pos = offset + jnp.arange(block_rows, dtype=jnp.int32)
            query_doc = lax.dynamic_slice_in_dim(documents, offset, block_rows, 0)
            allowed = (documents[None, :] == query_doc[:, None]) & (positions[None, :] <= query_pos[:, None])
            scores = jnp.dot(query_rows, key_cols.T, preferred_element_type=jnp.float32) * scale
            scores = jnp.where(allowed, scores, -1e30)
            highest = jnp.max(scores, axis=1, keepdims=True)
            weights = jnp.where(allowed, jnp.exp(scores - highest), 0.0)
            total = jnp.sum(weights, axis=1, keepdims=True)
            mixed = jnp.dot(weights.astype(jnp.bfloat16), value_cols, preferred_element_type=jnp.float32)
            return mixed / total

        return lax.map(one_block, jnp.arange(block_total, dtype=jnp.int32)).reshape(ROW_TOKENS, HEAD_SIZE)

    per_head = lax.map(one_head, jnp.arange(HQ, dtype=jnp.int32))
    attention = jnp.transpose(per_head, (1, 0, 2)).reshape(ROW_TOKENS, HQ * HEAD_SIZE).astype(jnp.bfloat16)
    ordering = jnp.argsort(mlp_owner, stable=True)
    routed = attention[ordering]
    projected = jnp.dot(routed, out_weight, preferred_element_type=jnp.float32)
    return (projected + residual.astype(jnp.float32)).astype(jnp.bfloat16)
```

```python
import functools

import jax
import jax.numpy as jnp
from jax import lax
from jax.experimental import pallas as pl
from jax.experimental.pallas import tpu as pltpu
from jax.sharding import PartitionSpec as P

HEAD_SIZE = 128
GROUP = 4


neg_large = -1e30


def doc_index(positions, doc_ends):
    return jnp.sum((positions[:, None] >= doc_ends[None, :]).astype(jnp.int32), axis=1)


def mask_for(row_count, query_pos, query_doc, doc_ends):
    key_pos = jnp.arange(row_count, dtype=jnp.int32)
    key_doc = doc_index(key_pos, doc_ends)
    return (key_doc[None, :] == query_doc[:, None]) & (key_pos[None, :] <= query_pos[:, None])


def attend(running, key_piece, value_piece, allowed, query_heads):
    running_max, running_sum, accumulated = running
    scores = jnp.einsum(
        "qhd,kd->hqk", query_heads, key_piece, preferred_element_type=jnp.float32
    ) * HEAD_SIZE ** (-0.5)
    scores = jnp.where(allowed[None], scores, neg_large)
    new_max = jnp.maximum(running_max, jnp.max(scores, axis=2))
    weights = jnp.where(allowed[None], jnp.exp(scores - new_max[:, :, None]), 0.0)
    new_sum = jnp.sum(weights, axis=2)
    update = jnp.einsum(
        "hqk,kd->hqd", weights.astype(jnp.bfloat16), value_piece, preferred_element_type=jnp.float32
    )
    return (new_max, new_sum, update)


def per_device(queries, keys, values, lengths, mlp_owner, out_weight, residual):
    rows_here, columns = queries.shape
    heads_here = columns // HEAD_SIZE
    dc_count = lax.axis_size("dc")
    dc_index = lax.axis_index("dc")
    tp_index = lax.axis_index("tp")
    kv_group = tp_index * heads_here // GROUP
    key_head = lax.dynamic_slice_in_dim(keys, kv_group * HEAD_SIZE, HEAD_SIZE, 1)
    value_head = lax.dynamic_slice_in_dim(values, kv_group * HEAD_SIZE, HEAD_SIZE, 1)
    order = jnp.arange(lengths.shape[0], dtype=jnp.int32)
    doc_ends = jnp.sum(jnp.where(order[None, :] <= order[:, None], lengths[None, :], 0), axis=1)
    local_rows = jnp.arange(rows_here, dtype=jnp.int32)
    query_pos = dc_index * rows_here + local_rows
    own_targets = lax.dynamic_slice_in_dim(mlp_owner, dc_index * rows_here, rows_here, 0)
    spread = 1
    query_doc = doc_index(query_pos, doc_ends)
    query_heads = queries.reshape(rows_here, heads_here, HEAD_SIZE)
    initial = (
        jnp.full((heads_here, rows_here), neg_large, jnp.float32),
        jnp.zeros((heads_here, rows_here), jnp.float32),
        jnp.zeros((heads_here, rows_here, HEAD_SIZE), jnp.float32),
    )
    key_piece = lax.all_gather(key_head, "dc", axis=0, tiled=True)
    value_piece = lax.all_gather(value_head, "dc", axis=0, tiled=True)
    allowed = mask_for(key_piece.shape[0], query_pos, query_doc, doc_ends)

    def compute():
        return attend(initial, key_piece, value_piece, allowed, query_heads)

    def unchanged():
        return initial

    outcome = lax.cond(jnp.any(allowed), compute, unchanged)
    running_max, running_sum, accumulated = outcome
    attention = (accumulated / running_sum[:, :, None]).astype(jnp.bfloat16)
    attention = jnp.transpose(attention, (1, 0, 2)).reshape(rows_here, columns)
    capacity = spread * ((rows_here + dc_count - 1) // dc_count + rows_here // dc_count)
    slot_total = dc_count * capacity
    earlier = local_rows[None, :] < local_rows[:, None]
    same_target = own_targets[None, :] == own_targets[:, None]
    slot_rank = jnp.sum((same_target & earlier).astype(jnp.int32), axis=1)
    slot_index = own_targets * capacity + slot_rank
    slot_ids = jnp.arange(slot_total, dtype=jnp.int32)
    placement = (slot_ids[:, None] == slot_index[None, :]).astype(jnp.bfloat16)
    outgoing = jnp.dot(placement, attention, preferred_element_type=jnp.float32).astype(
        jnp.bfloat16
    )
    outgoing = outgoing.reshape(dc_count, capacity, columns)
    incoming = lax.all_to_all(outgoing, "dc", split_axis=0, concat_axis=0, tiled=True)
    mine_blocks = (mlp_owner == dc_index).astype(jnp.bfloat16).reshape(dc_count, rows_here)
    lower_ones = (local_rows[:, None] <= local_rows[None, :]).astype(jnp.bfloat16)
    within_prefix = jnp.dot(mine_blocks, lower_ones, preferred_element_type=jnp.float32).astype(
        jnp.int32
    )
    block_counts = within_prefix[:, rows_here - 1]
    block_ids = jnp.arange(dc_count, dtype=jnp.int32)
    block_start = jnp.sum(
        jnp.where(block_ids[None, :] < block_ids[:, None], block_counts[None, :], 0), axis=1
    )
    mine_flat = mine_blocks.reshape(dc_count * rows_here) > 0
    rank_flat = (block_start[:, None] + within_prefix - 1).reshape(dc_count * rows_here)
    rank_flat = jnp.where(mine_flat, rank_flat, -1)
    all_pos = jnp.arange(dc_count * rows_here, dtype=jnp.int32)
    token_ids = jnp.sum(
        jnp.where(rank_flat[None, :] == local_rows[:, None], all_pos[None, :], 0), axis=1
    )
    token_slab = token_ids // rows_here
    token_within = token_ids % rows_here
    token_holder = jnp.where(token_within < rows_here, token_slab, dc_count - 1 - token_slab)
    same_holder = token_holder[None, :] == token_holder[:, None]
    before_here = token_within[None, :] < token_within[:, None]
    held_rank = jnp.sum((same_holder & before_here).astype(jnp.int32), axis=1)
    token_slots = token_holder * capacity + held_rank
    chooser = (token_slots[:, None] == slot_ids[None, :]).astype(jnp.bfloat16)
    incoming_flat = incoming.reshape(slot_total, columns)
    owned_rows = jnp.dot(chooser, incoming_flat, preferred_element_type=jnp.float32).astype(
        jnp.bfloat16
    )
    summed = lax.psum_scatter(
        jnp.dot(owned_rows, out_weight, preferred_element_type=jnp.float32).astype(jnp.bfloat16),
        "tp",
        scatter_dimension=0,
        tiled=True,
    ).astype(jnp.float32)
    return (summed + residual.astype(jnp.float32)).astype(jnp.bfloat16)


MESH = pl.DeviceIdType.MESH
SHARERS = 2
COLUMN_CHUNK = 256


def fused(dc_count, tp_count, lengths, owners, queries, keys, values, weight, out,
          key_all, value_all, attn, outgoing, incoming, rows_all, weight_cols, finished,
          kv_send, kv_recv, route_send, route_recv, share_send, share_recv,
          weight_send, weight_recv, pass_send, pass_recv, own_sem, out_send, out_recv):
    rows, columns = queries.shape
    heads = columns // HEAD_SIZE
    depth, width = weight.shape
    my_width = width // tp_count
    quarter = rows // tp_count
    capacity = incoming.shape[0] // dc_count
    total = dc_count * rows
    part = depth // SHARERS
    me, tp = lax.axis_index("dc"), lax.axis_index("tp")
    group = tp * heads // GROUP
    head_cols = pl.ds(pl.multiple_of(group * HEAD_SIZE, HEAD_SIZE), HEAD_SIZE)
    lane = lax.rem(me, SHARERS)
    base = me - lane

    def remote(src, dst, send, recv, **where):
        return pltpu.make_async_remote_copy(
            src_ref=src, dst_ref=dst, send_sem=send, recv_sem=recv,
            device_id=where, device_id_type=MESH)

    barrier = pltpu.get_barrier_semaphore()
    for o in range(1, dc_count):
        pl.semaphore_signal(barrier, inc=1, device_id={"dc": lax.rem(me + o, dc_count)}, device_id_type=MESH)
    for o in range(1, tp_count):
        pl.semaphore_signal(barrier, inc=1, device_id={"tp": lax.rem(tp + o, tp_count)}, device_id_type=MESH)
    pl.semaphore_wait(barrier, dc_count + tp_count - 2)

    def kv_copies(o, slab, peer):
        at = pl.ds(pl.multiple_of(slab * rows, rows), rows)
        return (
            remote(keys.at[:, head_cols], key_all.at[at], kv_send.at[o, 0], kv_recv.at[o, 0], dc=peer),
            remote(values.at[:, head_cols], value_all.at[at], kv_send.at[o, 1], kv_recv.at[o, 1], dc=peer),
        )

    for o in range(1, dc_count):
        @pl.when(me + o < dc_count)
        def _():
            for copy in kv_copies(o, me, me + o):
                copy.start()

    my_part = pl.ds(pl.multiple_of(lane * part, part), part)

    def weight_copy(o, source, peer):
        return remote(weight.at[my_part, pl.ds(pl.multiple_of(peer * my_width, my_width), my_width)],
                      weight_cols.at[source, my_part], weight_send.at[o], weight_recv.at[o], tp=peer)

    for o in range(1, tp_count):
        weight_copy(o, tp, lax.rem(tp + o, tp_count)).start()
    own = pltpu.make_async_copy(
        weight.at[:, pl.ds(pl.multiple_of(tp * my_width, my_width), my_width)], weight_cols.at[tp], own_sem)
    own.start()

    mine = pl.ds(pl.multiple_of(me * rows, rows), rows)
    key_all[mine, :] = keys[:, head_cols]
    value_all[mine, :] = values[:, head_cols]
    for o in range(1, dc_count):
        @pl.when(me + o < dc_count)
        def _():
            later = pl.ds(pl.multiple_of((me + o) * rows, rows), rows)
            key_all[later, :] = jnp.zeros((rows, HEAD_SIZE), key_all.dtype)
            value_all[later, :] = jnp.zeros((rows, HEAD_SIZE), value_all.dtype)

    position = me * rows + lax.broadcasted_iota(jnp.int32, (rows, 1), 0)
    first = jnp.zeros((rows, 1), jnp.int32)
    end = jnp.int32(0)
    for k in range(lengths.shape[0]):
        end = end + lengths[k]
        first = jnp.where(position >= end, end, first)

    my_targets = owners[pl.ds(me, 1), :]
    hot = (lax.broadcasted_iota(jnp.int32, (dc_count, rows), 0) == my_targets)
    before = (lax.broadcasted_iota(jnp.int32, (rows, rows), 0)
              < lax.broadcasted_iota(jnp.int32, (rows, rows), 1)).astype(jnp.float32).astype(jnp.bfloat16)
    hot_f = hot.astype(jnp.float32)
    prefix = jnp.dot(hot_f.astype(jnp.bfloat16), before, preferred_element_type=jnp.float32)
    rank = jnp.sum(hot_f * prefix, axis=0, keepdims=True)
    slot = my_targets.astype(jnp.float32) * capacity + rank
    slot_ids = lax.broadcasted_iota(jnp.int32, (dc_count * capacity, rows), 0).astype(jnp.float32)
    placement = jnp.where(slot_ids == slot, 1.0, 0.0).astype(jnp.bfloat16)

    counts = jnp.sum((owners[...] == me).astype(jnp.float32), axis=1, keepdims=True)
    slots = lax.broadcasted_iota(jnp.int32, (1, dc_count * capacity), 1).astype(jnp.float32)
    goal = jnp.full((1, dc_count * capacity), -1.0, jnp.float32)
    begin = jnp.zeros((1, 1), jnp.float32)
    for s in range(dc_count):
        held = counts[s : s + 1, :]
        k = slots - float(s * capacity)
        goal = jnp.where((k >= 0.0) & (k < held), begin + k, goal)
        begin = begin + held
    out_rows = lax.broadcasted_iota(jnp.int32, (rows, dc_count * capacity), 0).astype(jnp.float32)
    chooser = jnp.where(out_rows == goal, 1.0, 0.0).astype(jnp.bfloat16)

    for o in range(1, dc_count):
        @pl.when(me - o >= 0)
        def _():
            for copy in kv_copies(o, me - o, me):
                copy.wait_recv()

    key_pos = lax.broadcasted_iota(jnp.int32, (rows, total), 1)
    allowed = (key_pos >= first) & (key_pos <= position)
    for h in range(heads):
        cols = slice(h * HEAD_SIZE, (h + 1) * HEAD_SIZE)
        scores = lax.dot_general(queries[:, cols], key_all[...], (((1,), (1,)), ((), ())),
                                 preferred_element_type=jnp.float32) * HEAD_SIZE ** (-0.5)
        scores = jnp.where(allowed, scores, neg_large)
        weights = jnp.exp(scores - jnp.max(scores, axis=1, keepdims=True))
        weights = jnp.where(allowed, weights, 0.0)
        mixed = jnp.dot(weights.astype(jnp.bfloat16), value_all[...], preferred_element_type=jnp.float32)
        attn[:, cols] = (mixed / jnp.sum(weights, axis=1, keepdims=True)).astype(attn.dtype)

    outgoing[...] = jnp.dot(placement, attn[...], preferred_element_type=jnp.float32).astype(outgoing.dtype)

    def route_copy(o, source, peer):
        return remote(outgoing.at[pl.ds(pl.multiple_of(peer * capacity, capacity), capacity)],
                      incoming.at[pl.ds(pl.multiple_of(source * capacity, capacity), capacity)],
                      route_send.at[o], route_recv.at[o], dc=peer)

    for o in range(1, dc_count):
        route_copy(o, me, lax.rem(me + o, dc_count)).start()
    here = pl.ds(pl.multiple_of(me * capacity, capacity), capacity)
    incoming[here, :] = outgoing[here, :]

    def pass_copy(o, p, source, rows_at, peer):
        return remote(weight_cols.at[source, rows_at], weight_cols.at[source, rows_at],
                      pass_send.at[o, p], pass_recv.at[o, p], dc=peer)

    def pass_on(o):
        source = lax.rem(tp - o + tp_count, tp_count)
        weight_copy(o, source, tp).wait_recv()
        for p in range(1, SHARERS):
            pass_copy(o, p, source, my_part, base + lax.rem(lane + p, SHARERS)).start()

    for o in range(1, dc_count):
        route_copy(o, lax.rem(me - o + dc_count, dc_count), me).wait_recv()
    rows_all[tp] = jnp.dot(chooser, incoming[...], preferred_element_type=jnp.float32).astype(rows_all.dtype)

    def share_copy(o, source, peer):
        return remote(rows_all.at[source], rows_all.at[source], share_send.at[o], share_recv.at[o], tp=peer)

    for o in range(1, tp_count):
        share_copy(o, tp, lax.rem(tp + o, tp_count)).start()
    for o in range(1, tp_count):
        pass_on(o)
    own.wait()
    for o in range(1, tp_count):
        source = lax.rem(tp - o + tp_count, tp_count)
        share_copy(o, source, tp).wait_recv()
        for p in range(1, SHARERS):
            theirs = lax.rem(lane - p + SHARERS, SHARERS)
            at = pl.ds(pl.multiple_of(theirs * part, part), part)
            pass_copy(o, p, source, at, me).wait_recv()

    def out_copy(o, c, source, peer):
        return remote(finished.at[pl.ds(pl.multiple_of(peer * quarter, quarter), quarter),
                                  c * COLUMN_CHUNK : (c + 1) * COLUMN_CHUNK],
                      out.at[:, pl.ds(pl.multiple_of(source * my_width + c * COLUMN_CHUNK, COLUMN_CHUNK), COLUMN_CHUNK)],
                      out_send.at[o, c], out_recv.at[o, c], tp=peer)

    chunks = my_width // COLUMN_CHUNK
    for c in range(chunks):
        cols = slice(c * COLUMN_CHUNK, (c + 1) * COLUMN_CHUNK)
        acc = jnp.dot(rows_all[0], weight_cols[0, :, cols], preferred_element_type=jnp.float32)
        for r in range(1, tp_count):
            acc = acc + jnp.dot(rows_all[r], weight_cols[r, :, cols], preferred_element_type=jnp.float32)
        finished[:, cols] = acc.astype(finished.dtype)
        for o in range(1, tp_count):
            out_copy(o, c, tp, lax.rem(tp + o, tp_count)).start()
    keep = finished[pl.ds(pl.multiple_of(tp * quarter, quarter), quarter), :]
    out[:, pl.ds(pl.multiple_of(tp * my_width, my_width), my_width)] = keep

    for o in range(1, tp_count):
        for c in range(chunks):
            out_copy(o, c, lax.rem(tp - o + tp_count, tp_count), tp).wait_recv()
    for o in range(1, dc_count):
        @pl.when(me + o < dc_count)
        def _():
            for copy in kv_copies(o, me, me + o):
                copy.wait_send()
        route_copy(o, me, lax.rem(me + o, dc_count)).wait_send()
    for o in range(1, tp_count):
        peer = lax.rem(tp + o, tp_count)
        weight_copy(o, tp, peer).wait_send()
        share_copy(o, tp, peer).wait_send()
        for p in range(1, SHARERS):
            pass_copy(o, p, lax.rem(tp - o + tp_count, tp_count), my_part,
                      base + lax.rem(lane + p, SHARERS)).wait_send()
        for c in range(chunks):
            out_copy(o, c, tp, peer).wait_send()


def in_one_kernel(dc_count, tp_count, queries, keys, values, lengths, mlp_owner, out_weight, residual):
    rows, columns = queries.shape
    depth, width = out_weight.shape
    capacity = (rows + dc_count - 1) // dc_count + rows // dc_count
    chunks = width // tp_count // COLUMN_CHUNK
    half = jnp.bfloat16
    dma = pltpu.SemaphoreType.DMA
    vmem, smem = pl.BlockSpec(memory_space=pltpu.VMEM), pl.BlockSpec(memory_space=pltpu.SMEM)
    summed = pl.pallas_call(
        functools.partial(fused, dc_count, tp_count),
        out_shape=jax.ShapeDtypeStruct((rows // tp_count, width), half),
        in_specs=[smem, vmem, vmem, vmem, vmem, pl.BlockSpec(memory_space=pl.ANY)],
        out_specs=vmem,
        scratch_shapes=[
            pltpu.VMEM((dc_count * rows, HEAD_SIZE), half),
            pltpu.VMEM((dc_count * rows, HEAD_SIZE), half),
            pltpu.VMEM((rows, columns), half),
            pltpu.VMEM((dc_count * capacity, columns), half),
            pltpu.VMEM((dc_count * capacity, columns), half),
            pltpu.VMEM((tp_count, rows, columns), half),
            pltpu.VMEM((tp_count, depth, width // tp_count), half),
            pltpu.VMEM((rows, width // tp_count), half),
            dma((dc_count, 2)), dma((dc_count, 2)),
            dma((dc_count,)), dma((dc_count,)),
            dma((tp_count,)), dma((tp_count,)),
            dma((tp_count,)), dma((tp_count,)),
            dma((tp_count, SHARERS)), dma((tp_count, SHARERS)),
            dma(()),
            dma((tp_count, chunks)), dma((tp_count, chunks)),
        ],
        compiler_params=pltpu.CompilerParams(
            collective_id=0, has_side_effects=True, vmem_limit_bytes=40 * 2**20),
    )(lengths, mlp_owner.reshape(dc_count, rows), queries, keys, values, out_weight)
    return (summed.astype(jnp.float32) + residual.astype(jnp.float32)).astype(half)


def body(dc_count, tp_count, *arrays):
    queries, out_weight = arrays[0], arrays[5]
    rows, width = queries.shape[0], out_weight.shape[1]
    fits = (
        width % (tp_count * COLUMN_CHUNK) == 0
        and dc_count % SHARERS == 0
        and rows % (16 * tp_count) == 0
        and rows // dc_count * dc_count == rows
        and (2 * (rows // dc_count)) % 16 == 0
        and dc_count * rows <= 2048
    )
    if fits:
        return in_one_kernel(dc_count, tp_count, *arrays)
    return per_device(*arrays)


def solution(mesh):
    return jax.shard_map(
        functools.partial(body, mesh.shape["dc"], mesh.shape["tp"]),
        mesh=mesh,
        in_specs=(
            P("dc", "tp"),
            P("dc", None),
            P("dc", None),
            P(),
            P(),
            P("tp", None),
            P(("dc", "tp"), None),
        ),
        out_specs=P(("dc", "tp"), None),
        check_vma=False,
    )
```

```python
import functools

import jax
import jax.numpy as jnp
from jax import lax
from jax.experimental import pallas as pl
from jax.experimental.pallas import tpu as pltpu
from jax.sharding import PartitionSpec as P

HEAD_SIZE = 128
GROUP = 4


neg_large = -1e30


def doc_index(positions, doc_ends):
    return jnp.sum((positions[:, None] >= doc_ends[None, :]).astype(jnp.int32), axis=1)


def mask_for(row_count, query_pos, query_doc, doc_ends):
    key_pos = jnp.arange(row_count, dtype=jnp.int32)
    key_doc = doc_index(key_pos, doc_ends)
    return (key_doc[None, :] == query_doc[:, None]) & (key_pos[None, :] <= query_pos[:, None])


def attend(running, key_piece, value_piece, allowed, query_heads):
    running_max, running_sum, accumulated = running
    scores = jnp.einsum(
        "qhd,kd->hqk", query_heads, key_piece, preferred_element_type=jnp.float32
    ) * HEAD_SIZE ** (-0.5)
    scores = jnp.where(allowed[None], scores, neg_large)
    new_max = jnp.maximum(running_max, jnp.max(scores, axis=2))
    weights = jnp.where(allowed[None], jnp.exp(scores - new_max[:, :, None]), 0.0)
    new_sum = jnp.sum(weights, axis=2)
    update = jnp.einsum(
        "hqk,kd->hqd", weights.astype(jnp.bfloat16), value_piece, preferred_element_type=jnp.float32
    )
    return (new_max, new_sum, update)


def per_device(queries, keys, values, lengths, mlp_owner, out_weight, residual):
    rows_here, columns = queries.shape
    heads_here = columns // HEAD_SIZE
    dc_count = lax.axis_size("dc")
    dc_index = lax.axis_index("dc")
    tp_index = lax.axis_index("tp")
    kv_group = tp_index * heads_here // GROUP
    key_head = lax.dynamic_slice_in_dim(keys, kv_group * HEAD_SIZE, HEAD_SIZE, 1)
    value_head = lax.dynamic_slice_in_dim(values, kv_group * HEAD_SIZE, HEAD_SIZE, 1)
    order = jnp.arange(lengths.shape[0], dtype=jnp.int32)
    doc_ends = jnp.sum(jnp.where(order[None, :] <= order[:, None], lengths[None, :], 0), axis=1)
    local_rows = jnp.arange(rows_here, dtype=jnp.int32)
    query_pos = dc_index * rows_here + local_rows
    own_targets = lax.dynamic_slice_in_dim(mlp_owner, dc_index * rows_here, rows_here, 0)
    spread = 1
    query_doc = doc_index(query_pos, doc_ends)
    query_heads = queries.reshape(rows_here, heads_here, HEAD_SIZE)
    initial = (
        jnp.full((heads_here, rows_here), neg_large, jnp.float32),
        jnp.zeros((heads_here, rows_here), jnp.float32),
        jnp.zeros((heads_here, rows_here, HEAD_SIZE), jnp.float32),
    )
    key_piece = lax.all_gather(key_head, "dc", axis=0, tiled=True)
    value_piece = lax.all_gather(value_head, "dc", axis=0, tiled=True)
    allowed = mask_for(key_piece.shape[0], query_pos, query_doc, doc_ends)

    def compute():
        return attend(initial, key_piece, value_piece, allowed, query_heads)

    def unchanged():
        return initial

    outcome = lax.cond(jnp.any(allowed), compute, unchanged)
    running_max, running_sum, accumulated = outcome
    attention = (accumulated / running_sum[:, :, None]).astype(jnp.bfloat16)
    attention = jnp.transpose(attention, (1, 0, 2)).reshape(rows_here, columns)
    capacity = spread * ((rows_here + dc_count - 1) // dc_count + rows_here // dc_count)
    slot_total = dc_count * capacity
    earlier = local_rows[None, :] < local_rows[:, None]
    same_target = own_targets[None, :] == own_targets[:, None]
    slot_rank = jnp.sum((same_target & earlier).astype(jnp.int32), axis=1)
    slot_index = own_targets * capacity + slot_rank
    slot_ids = jnp.arange(slot_total, dtype=jnp.int32)
    placement = (slot_ids[:, None] == slot_index[None, :]).astype(jnp.bfloat16)
    outgoing = jnp.dot(placement, attention, preferred_element_type=jnp.float32).astype(
        jnp.bfloat16
    )
    outgoing = outgoing.reshape(dc_count, capacity, columns)
    incoming = lax.all_to_all(outgoing, "dc", split_axis=0, concat_axis=0, tiled=True)
    mine_blocks = (mlp_owner == dc_index).astype(jnp.bfloat16).reshape(dc_count, rows_here)
    lower_ones = (local_rows[:, None] <= local_rows[None, :]).astype(jnp.bfloat16)
    within_prefix = jnp.dot(mine_blocks, lower_ones, preferred_element_type=jnp.float32).astype(
        jnp.int32
    )
    block_counts = within_prefix[:, rows_here - 1]
    block_ids = jnp.arange(dc_count, dtype=jnp.int32)
    block_start = jnp.sum(
        jnp.where(block_ids[None, :] < block_ids[:, None], block_counts[None, :], 0), axis=1
    )
    mine_flat = mine_blocks.reshape(dc_count * rows_here) > 0
    rank_flat = (block_start[:, None] + within_prefix - 1).reshape(dc_count * rows_here)
    rank_flat = jnp.where(mine_flat, rank_flat, -1)
    all_pos = jnp.arange(dc_count * rows_here, dtype=jnp.int32)
    token_ids = jnp.sum(
        jnp.where(rank_flat[None, :] == local_rows[:, None], all_pos[None, :], 0), axis=1
    )
    token_slab = token_ids // rows_here
    token_within = token_ids % rows_here
    token_holder = jnp.where(token_within < rows_here, token_slab, dc_count - 1 - token_slab)
    same_holder = token_holder[None, :] == token_holder[:, None]
    before_here = token_within[None, :] < token_within[:, None]
    held_rank = jnp.sum((same_holder & before_here).astype(jnp.int32), axis=1)
    token_slots = token_holder * capacity + held_rank
    chooser = (token_slots[:, None] == slot_ids[None, :]).astype(jnp.bfloat16)
    incoming_flat = incoming.reshape(slot_total, columns)
    owned_rows = jnp.dot(chooser, incoming_flat, preferred_element_type=jnp.float32).astype(
        jnp.bfloat16
    )
    summed = lax.psum_scatter(
        jnp.dot(owned_rows, out_weight, preferred_element_type=jnp.float32).astype(jnp.bfloat16),
        "tp",
        scatter_dimension=0,
        tiled=True,
    ).astype(jnp.float32)
    return (summed + residual.astype(jnp.float32)).astype(jnp.bfloat16)


MESH = pl.DeviceIdType.MESH
SHARERS = 4
COLUMN_CHUNK = 256


def fused(dc_count, tp_count, lengths, owners, queries, keys, values, weight, out,
          query_own, kv_all, attn, outgoing, incoming, rows_all, weight_cols, finished,
          kv_send, kv_recv, hand_send, hand_recv, pair_send, pair_recv, route_send, route_recv, share_send, share_recv,
          weight_send, weight_recv, pass_send, pass_recv, own_sem, local_sem, out_send, out_recv):
    rows, columns = queries.shape
    heads = columns // HEAD_SIZE
    depth, width = weight.shape
    my_width = width // tp_count
    quarter = rows // tp_count
    capacity = incoming.shape[1] // dc_count
    total = dc_count * rows
    part = depth // SHARERS
    me, tp = lax.axis_index("dc"), lax.axis_index("tp")
    group = tp * heads // GROUP
    head_cols = pl.ds(pl.multiple_of(group * HEAD_SIZE, HEAD_SIZE), HEAD_SIZE)

    def remote(src, dst, send, recv, **where):
        return pltpu.make_async_remote_copy(
            src_ref=src, dst_ref=dst, send_sem=send, recv_sem=recv,
            device_id=where, device_id_type=MESH)

    mine = pl.ds(pl.multiple_of(me * rows, rows), rows)
    local = (
        pltpu.make_async_copy(keys.at[:, head_cols], kv_all.at[0, mine], local_sem.at[0]),
        pltpu.make_async_copy(values.at[:, head_cols], kv_all.at[1, mine], local_sem.at[1]),
        pltpu.make_async_copy(queries, query_own, local_sem.at[2]),
    )
    for copy in local:
        copy.start()
    own = pltpu.make_async_copy(
        weight.at[:, pl.ds(pl.multiple_of(tp * my_width, my_width), my_width)], weight_cols.at[tp], own_sem)
    own.start()

    barrier = pltpu.get_barrier_semaphore()
    for o in range(1, dc_count):
        pl.semaphore_signal(barrier, inc=1, device_id={"dc": lax.rem(me + o, dc_count)}, device_id_type=MESH)
    for o in range(1, tp_count):
        pl.semaphore_signal(barrier, inc=1, device_id={"tp": lax.rem(tp + o, tp_count)}, device_id_type=MESH)
    pl.semaphore_wait(barrier, dc_count + tp_count - 2)

    for copy in local:
        copy.wait()
    core = lax.rem(me, 2)
    pair = me - core
    other = pair + 1 - core

    def slab(index):
        return pl.ds(pl.multiple_of(index * rows, rows), rows)

    def kv_copy(first_of_pair, z, source):
        block = kv_all.at[z, slab(source)]
        return remote(block, block, kv_send.at[first_of_pair // 2, z], kv_recv.at[source], dc=first_of_pair + z)

    def pair_copy(z, source, peer):
        block = kv_all.at[z, slab(source)]
        return remote(block, block, pair_send.at[z], pair_recv.at[z], dc=peer)

    def hand_copy(z, source, peer):
        block = kv_all.at[z, slab(source)]
        return remote(block, block, hand_send.at[source], hand_recv.at[source], dc=peer)

    for p in range(2, dc_count, 2):
        @pl.when(pair < p)
        def _():
            for z in range(2):
                kv_copy(p, z, me).start()

    @pl.when(core == 0)
    def _():
        for z in range(2):
            pair_copy(z, me, me + 1).start()

    def sharing(o):
        stride = 2 if o % 2 == 1 else dc_count // 2
        bit = lax.rem(me // stride, 2)
        return core + 2 * bit, me - core - bit * stride, stride

    def part_of(lane):
        return pl.ds(pl.multiple_of(lane * part, part), part)

    def sharer(o, p):
        lane, origin, stride = sharing(o)
        there = lax.rem(lane + p, SHARERS)
        return origin + lax.rem(there, 2) + there // 2 * stride

    def weight_copy(o, source, peer):
        return remote(weight.at[part_of(sharing(o)[0]), pl.ds(pl.multiple_of(peer * my_width, my_width), my_width)],
                      weight_cols.at[source, part_of(sharing(o)[0])], weight_send.at[o], weight_recv.at[o], tp=peer)

    for o in range(1, tp_count):
        weight_copy(o, tp, lax.rem(tp + o, tp_count)).start()
    for o in range(1, dc_count):
        @pl.when(me + o < dc_count)
        def _():
            for z in range(2):
                kv_all[z, slab(me + o), :] = jnp.zeros((rows, HEAD_SIZE), kv_all.dtype)

    position = me * rows + lax.broadcasted_iota(jnp.int32, (rows, 1), 0)
    first = jnp.zeros((rows, 1), jnp.int32)
    end = jnp.int32(0)
    for k in range(lengths.shape[0]):
        end = end + lengths[k]
        first = jnp.where(position >= end, end, first)

    my_targets = owners[pl.ds(me, 1), :]
    hot = (lax.broadcasted_iota(jnp.int32, (dc_count, rows), 0) == my_targets)
    before = (lax.broadcasted_iota(jnp.int32, (rows, rows), 0)
              < lax.broadcasted_iota(jnp.int32, (rows, rows), 1)).astype(jnp.float32).astype(jnp.bfloat16)
    hot_f = hot.astype(jnp.float32)
    prefix = jnp.dot(hot_f.astype(jnp.bfloat16), before, preferred_element_type=jnp.float32)
    rank = jnp.sum(hot_f * prefix, axis=0, keepdims=True)
    slot = my_targets.astype(jnp.float32) * capacity + rank
    slot_ids = lax.broadcasted_iota(jnp.int32, (dc_count * capacity, rows), 0).astype(jnp.float32)
    placement = jnp.where(slot_ids == slot, 1.0, 0.0).astype(jnp.bfloat16)

    counts = jnp.sum((owners[...] == me).astype(jnp.float32), axis=1, keepdims=True)
    slots = lax.broadcasted_iota(jnp.int32, (1, dc_count * capacity), 1).astype(jnp.float32)
    goal = jnp.full((1, dc_count * capacity), -1.0, jnp.float32)
    begin = jnp.zeros((1, 1), jnp.float32)
    for s in range(dc_count):
        held = counts[s : s + 1, :]
        k = slots - float(s * capacity)
        goal = jnp.where((k >= 0.0) & (k < held), begin + k, goal)
        begin = begin + held
    out_rows = lax.broadcasted_iota(jnp.int32, (rows, dc_count * capacity), 0).astype(jnp.float32)
    chooser = jnp.where(out_rows == goal, 1.0, 0.0).astype(jnp.bfloat16)

    for source in range(dc_count - 2):
        @pl.when(source < pair)
        def _():
            kv_copy(0, core, source).wait_recv()
            hand_copy(core, source, other).start()

    @pl.when(core == 1)
    def _():
        for z in range(2):
            pair_copy(z, pair, me).wait_recv()

    for source in range(dc_count - 2):
        @pl.when(source < pair)
        def _():
            hand_copy(1 - core, source, me).wait_recv()

    def pass_copy(o, p, source, rows_at, peer):
        return remote(weight_cols.at[source, rows_at], weight_cols.at[source, rows_at],
                      pass_send.at[o, p], pass_recv.at[o, p], dc=peer)

    def pass_on(o):
        source = lax.rem(tp - o + tp_count, tp_count)
        weight_copy(o, source, tp).wait_recv()
        for p in range(1, SHARERS):
            pass_copy(o, p, source, part_of(sharing(o)[0]), sharer(o, p)).start()

    def route_copy(o, h, source, peer):
        return remote(outgoing.at[h, pl.ds(pl.multiple_of(peer * capacity, capacity), capacity)],
                      incoming.at[h, pl.ds(pl.multiple_of(source * capacity, capacity), capacity)],
                      route_send.at[o, h], route_recv.at[o, h], dc=peer)

    def share_copy(o, h, source, peer):
        return remote(rows_all.at[source, h], rows_all.at[source, h], share_send.at[o, h], share_recv.at[o, h], tp=peer)

    key_pos = lax.broadcasted_iota(jnp.int32, (rows, total), 1)
    allowed = (key_pos >= first) & (key_pos <= position)
    for h in range(heads):
        cols = slice(h * HEAD_SIZE, (h + 1) * HEAD_SIZE)
        scores = lax.dot_general(query_own[:, cols], kv_all[0], (((1,), (1,)), ((), ())),
                                 preferred_element_type=jnp.float32) * HEAD_SIZE ** (-0.5)
        scores = jnp.where(allowed, scores, neg_large)
        weights = jnp.exp(scores - jnp.max(scores, axis=1, keepdims=True))
        weights = jnp.where(allowed, weights, 0.0)
        mixed = jnp.dot(weights.astype(jnp.bfloat16), kv_all[1], preferred_element_type=jnp.float32)
        attn[h] = (mixed / jnp.sum(weights, axis=1, keepdims=True)).astype(attn.dtype)
        outgoing[h] = jnp.dot(placement, attn[h], preferred_element_type=jnp.float32).astype(outgoing.dtype)
        for o in range(1, dc_count):
            route_copy(o, h, me, lax.rem(me + o, dc_count)).start()
        here = pl.ds(pl.multiple_of(me * capacity, capacity), capacity)
        incoming[h, here, :] = outgoing[h, here, :]

    for o in range(1, tp_count):
        pass_on(o)

    for h in range(heads):
        for o in range(1, dc_count):
            route_copy(o, h, lax.rem(me - o + dc_count, dc_count), me).wait_recv()
        rows_all[tp, h] = jnp.dot(chooser, incoming[h], preferred_element_type=jnp.float32).astype(rows_all.dtype)
        for o in range(1, tp_count):
            share_copy(o, h, tp, lax.rem(tp + o, tp_count)).start()
    own.wait()
    for o in range(1, tp_count):
        source = lax.rem(tp - o + tp_count, tp_count)
        for h in range(heads):
            share_copy(o, h, source, tp).wait_recv()
        for p in range(1, SHARERS):
            theirs = lax.rem(sharing(o)[0] - p + SHARERS, SHARERS)
            pass_copy(o, p, source, part_of(theirs), me).wait_recv()

    def out_copy(o, c, source, peer):
        return remote(finished.at[pl.ds(pl.multiple_of(peer * quarter, quarter), quarter),
                                  c * COLUMN_CHUNK : (c + 1) * COLUMN_CHUNK],
                      out.at[:, pl.ds(pl.multiple_of(source * my_width + c * COLUMN_CHUNK, COLUMN_CHUNK), COLUMN_CHUNK)],
                      out_send.at[o, c], out_recv.at[o, c], tp=peer)

    chunks = my_width // COLUMN_CHUNK
    for c in range(chunks):
        cols = slice(c * COLUMN_CHUNK, (c + 1) * COLUMN_CHUNK)
        acc = jnp.zeros((rows, COLUMN_CHUNK), jnp.float32)
        for r in range(tp_count):
            together = jnp.concatenate([rows_all[r, h] for h in range(heads)], axis=1)
            acc = acc + jnp.dot(together, weight_cols[r, :, cols], preferred_element_type=jnp.float32)
        finished[:, cols] = acc.astype(finished.dtype)
        for o in range(1, tp_count):
            out_copy(o, c, tp, lax.rem(tp + o, tp_count)).start()
    keep = finished[pl.ds(pl.multiple_of(tp * quarter, quarter), quarter), :]
    out[:, pl.ds(pl.multiple_of(tp * my_width, my_width), my_width)] = keep

    for o in range(1, tp_count):
        for c in range(chunks):
            out_copy(o, c, lax.rem(tp - o + tp_count, tp_count), tp).wait_recv()
    for p in range(2, dc_count, 2):
        @pl.when(pair < p)
        def _():
            for z in range(2):
                kv_copy(p, z, me).wait_send()

    @pl.when(core == 0)
    def _():
        for z in range(2):
            pair_copy(z, me, me + 1).wait_send()

    for source in range(dc_count - 2):
        @pl.when(source < pair)
        def _():
            hand_copy(core, source, other).wait_send()

    for o in range(1, dc_count):
        for h in range(heads):
            route_copy(o, h, me, lax.rem(me + o, dc_count)).wait_send()
    for o in range(1, tp_count):
        peer = lax.rem(tp + o, tp_count)
        weight_copy(o, tp, peer).wait_send()
        for h in range(heads):
            share_copy(o, h, tp, peer).wait_send()
        for p in range(1, SHARERS):
            pass_copy(o, p, lax.rem(tp - o + tp_count, tp_count), part_of(sharing(o)[0]),
                      sharer(o, p)).wait_send()
        for c in range(chunks):
            out_copy(o, c, tp, peer).wait_send()


def in_one_kernel(dc_count, tp_count, queries, keys, values, lengths, mlp_owner, out_weight, residual):
    rows, columns = queries.shape
    depth, width = out_weight.shape
    heads = columns // HEAD_SIZE
    capacity = (rows + dc_count - 1) // dc_count + rows // dc_count
    chunks = width // tp_count // COLUMN_CHUNK
    half = jnp.bfloat16
    dma = pltpu.SemaphoreType.DMA
    vmem, smem = pl.BlockSpec(memory_space=pltpu.VMEM), pl.BlockSpec(memory_space=pltpu.SMEM)
    anywhere = pl.BlockSpec(memory_space=pl.ANY)
    summed = pl.pallas_call(
        functools.partial(fused, dc_count, tp_count),
        out_shape=jax.ShapeDtypeStruct((rows // tp_count, width), half),
        in_specs=[smem, vmem, anywhere, anywhere, anywhere, anywhere],
        out_specs=vmem,
        scratch_shapes=[
            pltpu.VMEM((rows, columns), half),
            pltpu.VMEM((2, dc_count * rows, HEAD_SIZE), half),
            pltpu.VMEM((heads, rows, HEAD_SIZE), half),
            pltpu.VMEM((heads, dc_count * capacity, HEAD_SIZE), half),
            pltpu.VMEM((heads, dc_count * capacity, HEAD_SIZE), half),
            pltpu.VMEM((tp_count, heads, rows, HEAD_SIZE), half),
            pltpu.VMEM((tp_count, depth, width // tp_count), half),
            pltpu.VMEM((rows, width // tp_count), half),
            dma((dc_count // 2, 2)), dma((dc_count,)),
            dma((dc_count,)), dma((dc_count,)),
            dma((2,)), dma((2,)),
            dma((dc_count, heads)), dma((dc_count, heads)),
            dma((tp_count, heads)), dma((tp_count, heads)),
            dma((tp_count,)), dma((tp_count,)),
            dma((tp_count, SHARERS)), dma((tp_count, SHARERS)),
            dma(()), dma((3,)),
            dma((tp_count, chunks)), dma((tp_count, chunks)),
        ],
        compiler_params=pltpu.CompilerParams(
            collective_id=0, has_side_effects=True, vmem_limit_bytes=60 * 2**20),
    )(lengths, mlp_owner.reshape(dc_count, rows), queries, keys, values, out_weight)
    return (summed.astype(jnp.float32) + residual.astype(jnp.float32)).astype(half)


def body(dc_count, tp_count, *arrays):
    queries, out_weight = arrays[0], arrays[5]
    rows, width = queries.shape[0], out_weight.shape[1]
    fits = (
        width % (tp_count * COLUMN_CHUNK) == 0
        and dc_count % SHARERS == 0
        and rows % (16 * tp_count) == 0
        and rows // dc_count * dc_count == rows
        and (2 * (rows // dc_count)) % 16 == 0
        and dc_count * rows <= 2048
    )
    if fits:
        return in_one_kernel(dc_count, tp_count, *arrays)
    return per_device(*arrays)


def solution(mesh):
    return jax.shard_map(
        functools.partial(body, mesh.shape["dc"], mesh.shape["tp"]),
        mesh=mesh,
        in_specs=(
            P("dc", "tp"),
            P("dc", None),
            P("dc", None),
            P(),
            P(),
            P("tp", None),
            P(("dc", "tp"), None),
        ),
        out_specs=P(("dc", "tp"), None),
        check_vma=False,
    )
```
